32 devices in a mesh: subj: 4 (over x, core), blk: 8 (over z, y).
Axes of the slice: x: 2, y: 2, z: 4, core: 2. Of those that a mesh axis runs over, the one named last changes fastest.
Arguments:
- series: bfloat16 [8, 1200, 8192], P('subj', None, 'blk'), may hold values from -170 to 170
- circle_step: int32 [1], replicated, may hold values from 1 to 7
- vertex_count: int32 [8], replicated, may hold values from 1 to 1024, 7168 in all
Outputs:
- group_z: float32 [1024, 8192], P('subj', 'blk')
The draws below stay inside these ranges and needn't reach their ends.
Inputs may be any that keep to these rules, and one draw needn't show every extreme that they name: `vertex_count`: the counts sum to 7168.
All inputs are finite; a program needn't handle non-finite values.
Results may differ from the reference program's by a relative error of at most 0.0019.
Values may be sent and summed in bfloat16 or wider, within the bound.
A program may use at most 192 MiB of HBM per device.

```python
import math
import jax
import jax.numpy as jnp
import numpy as np
from jax import lax

VB = 1024
FRAMES = 1200
SUBJECTS = 8
VERTS = 8192
N_BLK = 8


def draw_series(key, part):
    subkeys = jax.random.split(key, 5)
    full_shape = (SUBJECTS, FRAMES, VERTS)
    courses = jnp.clip(jax.random.normal(subkeys[0], (SUBJECTS, FRAMES, 2), jnp.float32), -4.0, 4.0)
    loadings = jax.random.uniform(subkeys[1], (SUBJECTS, 1, VERTS, 2), jnp.float32, -1.2, 1.2)
    noise = jnp.clip(jax.random.normal(subkeys[2], full_shape, jnp.float32), -4.0, 4.0)
    vertex_scale = jnp.exp(jax.random.uniform(subkeys[3], (SUBJECTS, 1, VERTS), jnp.float32, 0.0, math.log(10.0)))
    offset = jnp.clip(3.0 * jax.random.normal(subkeys[4], (SUBJECTS, 1, VERTS), jnp.float32), -9.0, 9.0)
    signal = courses[:, :, 0:1] * loadings[..., 0] + courses[:, :, 1:2] * loadings[..., 1] + noise
    return (signal * vertex_scale + offset).astype(jnp.bfloat16)


def split_up(number_of, total, reach, lean):
    loads = [(1 << 20) // math.isqrt(rank ** lean) + 1 for rank in range(2, number_of + 1)]
    surplus, holding = total - reach - (number_of - 1), [1] * (number_of - 1)
    while surplus > 0:
        movable = [i for i in range(number_of - 1) if holding[i] < reach]
        pool, budget = sum([loads[i] for i in movable]), surplus
        for i in movable:
            addition = min(reach - holding[i], max(1, budget * loads[i] // pool), surplus)
            holding[i] = holding[i] + addition
            surplus = surplus - addition
    return np.array([reach] + holding)


def ragged_sizes(key, count, total, reach, skew):
    if count == 2:
        one = jax.random.randint(key, (), max(1, total - reach), min(reach, total - 1) + 1)
        return jnp.stack([one, total - one])
    sizes = jnp.asarray(split_up(count, total, reach, skew), jnp.int32)
    twos = (count - 1) // 2
    giver, taker = sizes[1:1 + 2 * twos:2], sizes[2:2 + 2 * twos:2]
    room = jnp.minimum(giver - 1, reach - taker)
    shifted = jax.random.randint(jax.random.fold_in(key, 1), (twos,), 0, 1 << 20) % (room + 1)
    sizes = sizes.at[1:1 + 2 * twos:2].set(giver - shifted).at[2:2 + 2 * twos:2].set(taker + shifted)
    return sizes[jax.random.permutation(jax.random.fold_in(key, 2), count)]


def setup_inputs(seed: int = 0) -> dict:
    seeds = jax.random.split(jax.random.key(seed), 4)
    series = draw_series(jax.random.fold_in(seeds[3], 71), 0)
    circle_step = jax.random.randint(seeds[1], (1,), 1, N_BLK).astype(jnp.int32)
    vertex_count = ragged_sizes(seeds[2], N_BLK, N_BLK * VB - N_BLK * VB // 8, VB, 1).astype(jnp.int32)
    return {"series": series, "circle_step": circle_step, "vertex_count": vertex_count}


tr_seconds = 0.72
low_cut = 0.01
high_cut = 0.08
shrink = 0.98
epsilon = 1e-06

def tables(frames):
    index_row = jnp.arange(frames, dtype=jnp.int32)
    product_index = (2 * index_row[None, :] + 1) * index_row[:, None] % (4 * frames)
    phase_angle = product_index.astype(jnp.float32) * (math.pi / (2 * frames))
    row_scale = jnp.where(index_row == 0, math.sqrt(0.5), 1.0).astype(jnp.float32)
    cosine_table = jnp.cos(phase_angle) * math.sqrt(2.0 / frames) * row_scale[:, None]
    frequency = index_row.astype(jnp.float32) / (2 * frames * tr_seconds)
    high_pass = frequency / low_cut / jnp.sqrt(1.0 + (frequency / low_cut) ** 2)
    low_pass = 1.0 / jnp.sqrt(1.0 + (frequency / high_cut) ** 2)
    return (cosine_table.astype(jnp.bfloat16), (high_pass * low_pass)[:, None])

def normalize(raw_block, cosine_table, gains):
    coefficients = jnp.dot(cosine_table, raw_block, preferred_element_type=jnp.float32)
    weighted = (coefficients * gains).astype(jnp.bfloat16)
    filtered = jnp.dot(cosine_table.T, weighted, preferred_element_type=jnp.float32)
    frame_mean = lax.optimization_barrier(jnp.mean(filtered, axis=0, keepdims=True))
    centered = filtered - frame_mean
    variance = lax.optimization_barrier(jnp.mean(centered * centered, axis=0, keepdims=True))
    return (centered * lax.rsqrt(variance + epsilon)).astype(jnp.bfloat16)

def fisher(correlation):
    scaled = shrink * correlation
    return 0.5 * (jnp.log(1.0 + scaled) - jnp.log(1.0 - scaled))

def reference(series, circle_step, vertex_count):
    cosine_table, gains = tables(FRAMES)
    z_fields = jnp.stack([normalize(series[subject], cosine_table, gains) for subject in range(SUBJECTS)])
    shift_count = circle_step[0].astype(jnp.int32)

    def one_block(block):
        partner = ((block - shift_count) % N_BLK).astype(jnp.int32)
        own_z = lax.dynamic_slice_in_dim(z_fields, (block * VB).astype(jnp.int32), VB, 2)
        partner_z = lax.dynamic_slice_in_dim(z_fields, (partner * VB).astype(jnp.int32), VB, 2)
        running = jnp.zeros((VB, VB), jnp.float32)
        for subject in range(SUBJECTS):
            correlation = jnp.dot(partner_z[subject].T, own_z[subject], preferred_element_type=jnp.float32) / FRAMES
            running = running + fisher(correlation)
        slots = jnp.arange(VB, dtype=jnp.int32)
        keep_mask = (slots < vertex_count[partner])[:, None] & (slots < vertex_count[block])[None, :]
        return jnp.where(keep_mask, running / SUBJECTS, 0.0)
    tiles = lax.map(one_block, jnp.arange(N_BLK, dtype=jnp.int32))
    return jnp.transpose(tiles, (1, 0, 2)).reshape(VB, N_BLK * VB)
```

```python
import math

import jax
import jax.numpy as jnp
import numpy as np
from jax import lax
from jax.experimental import pallas as pl
from jax.experimental.pallas import tpu as pltpu
from jax.sharding import PartitionSpec as P

tr_seconds = 0.72
low_cut = 0.01
high_cut = 0.08
shrink = 0.98
epsilon = 1e-06
tile = 256
vmem_limit = 48 * 1024 * 1024


def tables(frames):
    index_row = np.arange(frames, dtype=np.int64)
    product_index = (2 * index_row[None, :] + 1) * index_row[:, None] % (4 * frames)
    phase_angle = product_index.astype(np.float64) * (math.pi / (2 * frames))
    row_scale = np.where(index_row == 0, math.sqrt(0.5), 1.0)
    cosine_table = np.cos(phase_angle) * math.sqrt(2.0 / frames) * row_scale[:, None]
    frequency = index_row.astype(np.float64) / (2 * frames * tr_seconds)
    high_pass = frequency / low_cut / np.sqrt(1.0 + (frequency / low_cut) ** 2)
    low_pass = 1.0 / np.sqrt(1.0 + (frequency / high_cut) ** 2)
    cosine_table = cosine_table.astype(jnp.bfloat16)
    gains = (high_pass * low_pass).astype(np.float32)[:, None]
    return cosine_table, np.ascontiguousarray(cosine_table.T), gains


def normalize(raw, table, table_t, gains):
    coefficients = jnp.dot(table, raw, preferred_element_type=jnp.float32)
    weighted = (coefficients * gains).astype(jnp.bfloat16)
    filtered = jnp.dot(table_t, weighted, preferred_element_type=jnp.float32)
    frames = filtered.shape[0]
    frame_mean = jnp.sum(filtered, axis=0, keepdims=True) * (1.0 / frames)
    centered = filtered - frame_mean
    variance = jnp.sum(centered * centered, axis=0, keepdims=True) * (1.0 / frames)
    return (centered * lax.rsqrt(variance + epsilon)).astype(jnp.bfloat16)


def own_kernel(raw_ref, table_ref, table_t_ref, gains_ref, z_ref):
    z_ref[0] = normalize(raw_ref[0], table_ref[...], table_t_ref[...], gains_ref[...])


def partner_kernel(raw_ref, own_ref, table_ref, table_t_ref, gains_ref, out_ref, z_scr):
    subjects, frames, _ = raw_ref.shape
    width = own_ref.shape[2]
    for subject in range(subjects):
        z_scr[subject] = normalize(
            raw_ref[subject], table_ref[...], table_t_ref[...], gains_ref[...]
        ).T
    for col in range(0, width, tile):
        above = None
        below = None
        for subject in range(subjects):
            correlation = jnp.dot(
                z_scr[subject],
                own_ref[subject, :, col : col + tile],
                preferred_element_type=jnp.float32,
            )
            scaled = correlation * (shrink / frames)
            above = 1.0 + scaled if above is None else above * (1.0 + scaled)
            below = 1.0 - scaled if below is None else below * (1.0 - scaled)
        out_ref[:, col : col + tile] = 0.5 * jnp.log(above / below)


def normalize_own(series, table, table_t, gains):
    subjects, frames, width = series.shape
    whole = lambda array: pl.BlockSpec(array.shape, lambda s, c: (0, 0))
    block = pl.BlockSpec((1, frames, tile), lambda s, c: (s, 0, c))
    return pl.pallas_call(
        own_kernel,
        grid=(subjects, width // tile),
        in_specs=[block, whole(table), whole(table_t), whole(gains)],
        out_specs=block,
        out_shape=jax.ShapeDtypeStruct(series.shape, jnp.bfloat16),
        compiler_params=pltpu.CompilerParams(vmem_limit_bytes=vmem_limit),
        cost_estimate=pl.CostEstimate(
            flops=4 * subjects * frames * frames * width,
            bytes_accessed=4 * series.size + 4 * frames * frames,
            transcendentals=0,
        ),
    )(series, table, table_t, gains)


def partner_rows(raw, own_z, table, table_t, gains):
    subjects, frames, rows = raw.shape
    width = own_z.shape[2]
    return pl.pallas_call(
        partner_kernel,
        in_specs=[pl.BlockSpec(memory_space=pltpu.VMEM)] * 5,
        out_specs=pl.BlockSpec(memory_space=pltpu.VMEM),
        out_shape=jax.ShapeDtypeStruct((rows, width), jnp.float32),
        scratch_shapes=[pltpu.VMEM((subjects, rows, frames), jnp.bfloat16)],
        compiler_params=pltpu.CompilerParams(vmem_limit_bytes=vmem_limit),
        cost_estimate=pl.CostEstimate(
            flops=subjects * rows * frames * (4 * frames + 2 * width),
            bytes_accessed=2 * raw.size + 2 * own_z.size + 4 * frames * frames + 4 * rows * width,
            transcendentals=rows * width,
        ),
    )(raw, own_z, table, table_t, gains)


def tile_rows(step, block_total, series, constants):
    pairs = [(source, (source + step) % block_total) for source in range(block_total)]
    width = series.shape[2]
    share = width // lax.axis_size("subj")
    chunks = [
        lax.ppermute(series[:, :, start : start + share], "blk", pairs)
        for start in range(0, width, share)
    ]
    own_z = normalize_own(series, *constants)
    core = lax.axis_index("subj") % 2
    core_pairs = [(0, 1), (1, 0), (2, 3), (3, 2)]
    sums = []
    for half in range(2):
        even, odd = (
            partner_rows(chunks[2 * half + part], own_z, *constants) for part in range(2)
        )
        kept = jnp.where(core == 0, even, odd)
        given = jnp.where(core == 0, odd, even)
        sums.append(kept + lax.ppermute(given, "subj", core_pairs))
    return sums


def local(series, circle_step, vertex_count):
    subj_local, frames, width = series.shape
    constants = [jnp.asarray(table) for table in tables(frames)]
    block_total = lax.axis_size("blk")
    subj_total = lax.axis_size("subj")
    subj_index = lax.axis_index("subj")
    own_block = lax.axis_index("blk")
    partner = (own_block - circle_step[0]) % block_total

    def branch(step):
        return lambda raw: tile_rows(step, block_total, raw, constants)

    low, high = lax.switch(
        circle_step[0] - 1, [branch(step) for step in range(1, block_total)], series
    )
    on_low = subj_index < 2
    given = jnp.where(on_low, high, low).astype(jnp.bfloat16)
    kept = jnp.where(on_low, low, high)
    taken = lax.ppermute(given, "subj", [(0, 2), (1, 3), (2, 0), (3, 1)])
    summed = kept + taken.astype(jnp.float32)
    row_share = width // subj_total
    block_ids = jnp.arange(block_total, dtype=jnp.int32)
    own_count = jnp.sum(jnp.where(block_ids == own_block, vertex_count, 0))
    partner_count = jnp.sum(jnp.where(block_ids == partner, vertex_count, 0))
    row_slots = subj_index * row_share + jnp.arange(row_share, dtype=jnp.int32)
    col_slots = jnp.arange(width, dtype=jnp.int32)
    keep_mask = (row_slots < partner_count)[:, None] & (col_slots < own_count)[None, :]
    return jnp.where(keep_mask, summed / (subj_local * subj_total), 0.0)


def solution(mesh):
    in_specs = (P("subj", None, "blk"), P(), P())
    out_specs = P("subj", "blk")
    return jax.shard_map(local, mesh=mesh, in_specs=in_specs, out_specs=out_specs, check_vma=False)
```
